32 devices in a mesh: row: 4 (over y, x), col: 8 (over z, core).
Axes of the slice: x: 2, y: 2, z: 4, core: 2. Of those that a mesh axis runs over, the one named last changes fastest.
Arguments:
- g_start: float32 [2048, 32768], P('row', 'col'), may hold values from -6 to 6
- cotangent: float32 [2048, 32768], P('row', 'col'), may hold values from -6 to 6
- damping: float32 [32768], replicated, may hold values from 0.1 to 3
- hopping: float32 [6, 32768], replicated, may hold values from -4 to 4
- bonds: int32 [7, 32768], replicated, may hold values 0 or 1
- source: float32 [7, 32768], replicated, may hold values from -5 to 5
Outputs:
- g_end: float32 [2048, 32768], P('row', 'col')
- g_adjoint: float32 [2048, 32768], P('row', 'col')
The draws below stay inside these ranges and needn't reach their ends.
All inputs are finite; a program needn't handle non-finite values.
Results may differ from the reference program's by a relative error of at most 0.00002.
Values sent between devices are 32-bit elements; how exact they have to be, the bound alone decides.
No kernel may reach another device: no remote copies, remote signals or barrier semaphores. Data moves between devices by JAX's collectives and lax.ppermute only.
A program may use at most 192 MiB of HBM per device.

```python
import math
import jax
import jax.numpy as jnp

LX = 128
BANDS = 7
MODES = 32768
ROWS = 2048


def touch_ends(drawn, stream_key, low, high):
    index_at = [jax.random.randint(jax.random.fold_in(stream_key, axis), (), 0, length) for axis, length in enumerate(drawn.shape)]
    main_axis = drawn.shape.index(max(drawn.shape))
    neighbour = index_at[:main_axis] + [(index_at[main_axis] + 1) % drawn.shape[main_axis]] + index_at[main_axis + 1:]
    return drawn.at[tuple(index_at)].set(low).at[tuple(neighbour)].set(high)


def levels(key, shape, pieces, low, largest):
    def one(dim, parts):
        steps = jax.random.uniform(jax.random.fold_in(jax.random.fold_in(key, 6), dim), (parts,), jnp.float32, low / len(pieces), largest / len(pieces))
        return jnp.repeat(jnp.exp(steps), shape[dim] // parts).reshape((-1,) + (1,) * (len(shape) - dim - 1))

    factor_of = one(*pieces[0])
    for cut in pieces[1:]:
        factor_of = factor_of * one(*cut)
    return factor_of


def normal_values(rng, shape, scale, most, split=(), kind=jnp.bfloat16):
    values = scale * jax.random.normal(rng, shape, jnp.float32)
    if split:
        values = values * levels(rng, shape, split, -0.22, 0.18)
    return jnp.clip(values, -most, most).astype(kind)


def setup_inputs(seed: int = 0) -> dict:
    arg_keys = jax.random.split(jax.random.key(seed), 7)
    g_start = normal_values(arg_keys[0], (ROWS, MODES), 1.0, 6.0, ((0, 4), (1, 8)), jnp.float32)
    cotangent = normal_values(arg_keys[1], (ROWS, MODES), 1.0, 6.0, ((0, 4), (1, 8)), jnp.float32)
    damping = jnp.clip(jnp.exp(jax.random.uniform(arg_keys[2], (MODES,), jnp.float32, math.log(0.1), math.log(3.0))), 0.1, 3.0)
    hopping = normal_values(arg_keys[3], (BANDS - 1, MODES), 1.0, 4.0, (), jnp.float32)
    bonds = touch_ends((jax.random.randint(arg_keys[4], (BANDS, MODES), 0, 4) < 3).astype(jnp.int32), jax.random.fold_in(arg_keys[4], 1), 0, 1)
    source = normal_values(arg_keys[5], (BANDS, MODES), 1.0, 5.0, (), jnp.float32)
    return {"g_start": g_start, "cotangent": cotangent, "damping": damping, "hopping": hopping, "bonds": bonds, "source": source}


DT = 0.1


def band_offsets(side):
    return (0, 1, -1, 2, -2, 2 * side, -2 * side)


def row_shift(field, offset):
    count = field.shape[1]
    if offset > 0:
        return jnp.concatenate([field[offset:], jnp.zeros((offset, count), jnp.float32)], axis=0)
    if offset < 0:
        return jnp.concatenate([jnp.zeros((-offset, count), jnp.float32), field[:offset]], axis=0)
    return field


def forward_rate(field, coef, source):
    rows = field.shape[0]
    modes = field.shape[1]
    row_ids = jnp.arange(rows, dtype=jnp.int32)
    total = jnp.zeros(field.shape, jnp.float32)
    for index, offset in enumerate(band_offsets(LX)):
        total = total + coef[index, :rows][:, None] * row_shift(field, offset)
        total = total + jnp.roll(field, -offset, axis=1) * coef[index][None, :]
        total = total.at[row_ids, jnp.mod(row_ids + offset, modes).astype(jnp.int32)].add(source[index, :rows])
    return total


def adjoint_rate(field, coef):
    rows = field.shape[0]
    total = jnp.zeros(field.shape, jnp.float32)
    for index, offset in enumerate(band_offsets(LX)):
        total = total + row_shift(coef[index, :rows][:, None] * field, -offset)
        total = total + jnp.roll(field * coef[index][None, :], offset, axis=1)
    return total


def reference(g_start, cotangent, damping, hopping, bonds, source):
    coef = jnp.concatenate([-damping[None, :], hopping], axis=0) * bonds.astype(jnp.float32)
    g_middle = g_start + 0.5 * DT * forward_rate(g_start, coef, source)
    g_end = g_start + DT * forward_rate(g_middle, coef, source)
    c_middle = cotangent + 0.5 * DT * adjoint_rate(cotangent, coef)
    g_adjoint = cotangent + DT * adjoint_rate(c_middle, coef)
    return g_end, g_adjoint
```

```python
import functools

import jax
import jax.numpy as jnp
from jax import lax
from jax.experimental import pallas as pl
from jax.experimental.pallas import tpu as pltpu
from jax.sharding import PartitionSpec as P

LX = 128
DT = 0.1

LANES = 128
STRIP = 8
REACH = 2 * LX
HALVES = REACH // LANES
UNROLL = 64
OFFSETS = (0, 1, -1, 2, -2, REACH, -REACH)
MIRROR = (0, 2, 1, 4, 3, 6, 5)
IN_FLIGHT = 2
HOLD = 5
VMEM = 28 * 2**20


def block_rates(win, lane, count, row, coef, coef_row, band, index, put):
    lanes = lax.broadcasted_iota(jnp.int32, (STRIP, LANES), 1)
    wide = count * HALVES

    def strip(i, _):
        at = pl.multiple_of(row + i * STRIP, STRIP)
        rows_c = pl.ds(pl.multiple_of(coef_row + i * STRIP, STRIP), STRIP)
        weights = [coef[k, rows_c, :] for k in range(7)]

        def load(j, shift=0):
            return win[lane + j, pl.ds(at + shift, STRIP), :]

        line = [load(j) for j in range(-1, wide + 1)]

        def moved(shift):
            if shift > 0:
                turned = [pltpu.roll(v, LANES - shift, 1) for v in line[1:]]
                return [jnp.where(lanes < LANES - shift, turned[c], turned[c + 1]) for c in range(wide)]
            turned = [pltpu.roll(v, -shift, 1) for v in line[:-1]]
            return [jnp.where(lanes >= -shift, turned[c + 1], turned[c]) for c in range(wide)]

        by_col = {s: moved(s) for s in (1, -1, 2, -2)}
        by_col[REACH] = [load(c + HALVES) for c in range(wide)]
        by_col[-REACH] = [load(c - HALVES) for c in range(wide)]
        for c in range(wide):
            value = line[c + 1]
            total = (weights[0] + band[index + c, 0]) * value
            for k in range(1, 7):
                total = total + weights[k] * load(c, OFFSETS[k])
                total = total + band[index + c, k] * by_col[OFFSETS[k]][c]
            put(c, i, value, total)
        return 0

    lax.fori_loop(0, REACH // STRIP, strip, 0, unroll=max(UNROLL // wide, 1))


def runs(tiles):
    found = []
    for tile in tiles:
        if found and tile == found[-1][0] + found[-1][1]:
            found[-1] = (found[-1][0], found[-1][1] + 1)
        else:
            found.append((tile, 1))
    return found


def tile_kernel(plan, *refs):
    names, a_own, a_near, b, own_loads, near_loads, far_loads, mid_loads, e_first, m_first, modes, cols, fed = plan
    n_in, n_out = len(names), len(a_own) + (1 if b else 0)
    ref = dict(zip(names, refs[:n_in]))
    outs = refs[n_in : n_in + n_out]
    win, mid, coef, band, feed, sems, out_sems, feed_sems = refs[n_in + n_out :]
    base = ref["base"][0]
    row_axis = lax.axis_index("row")
    odd = lax.rem(row_axis, 2)
    block_of = {"PF": 5 - 5 * odd, "PN": 4 - 3 * odd, "QN": 1 + 3 * odd, "QF": 5 * odd}
    row_first = row_axis * (2 * REACH)
    col_first = lax.axis_index("col") * cols
    own_rows = pl.ds(2 * REACH, 2 * REACH)
    mid_rows = pl.ds(REACH, 2 * REACH)
    used = []

    def load(src, dst):
        copy = pltpu.make_async_copy(src, dst, sems.at[len(used)])
        copy.start()
        used.append(copy)
        return copy

    def pair(first):
        return pl.ds(first * HALVES, HALVES)

    def load_piece(kind, name, offset, tile, group):
        start = pl.multiple_of(block_of[kind] * REACH, REACH)
        for c in range(HALVES):
            src = ref[name].at[pl.ds((offset + c) * REACH, REACH), :]
            group.append(load(src, win.at[(tile - e_first) * HALVES + c, pl.ds(start, REACH), :]))

    band_tiles = sorted(set(a_own) | set(a_near) | set(b))
    first, second, third = [], [], []
    for name, at, from_base, tile in own_loads:
        for c in range(HALVES):
            lane = at * REACH + c * LANES
            if from_base:
                lane = pl.multiple_of(base * REACH + lane, LANES)
            src = ref[name].at[:, pl.ds(lane, LANES)]
            first.append(load(src, win.at[(tile - e_first) * HALVES + c, own_rows, :]))
    for index, tile in enumerate(band_tiles):
        src = ref["band"].at[pl.ds((base + tile + 1) * HALVES, HALVES)]
        first.append(load(src, band.at[pair(index)]))
    if a_own or b:
        first.append(load(ref["coef"].at[:, mid_rows, :], coef.at[:, mid_rows, :]))
    for kind, name, offset, tile in near_loads:
        load_piece(kind, name, offset, tile, first if tile in a_own else second)
    for kind, name, offset, tile in far_loads:
        load_piece(kind, name, offset, tile, second)
    if a_near:
        for rows in (pl.ds(0, REACH), pl.ds(3 * REACH, REACH)):
            second.append(load(ref["coef"].at[:, rows, :], coef.at[:, rows, :]))
    for name, tile in mid_loads:
        third.append(load(ref[name], mid.at[pair(tile - m_first), mid_rows, :]))

    def wait(copies):
        for copy in copies:
            copy.wait()

    feeds = {}

    def load_source(stage, tile, block):
        ahead = col_first + (base + tile) * REACH - (row_first + (block - 1) * REACH)
        ahead = lax.rem(ahead + 2 * modes, modes)
        ahead = jnp.where(ahead * 2 > modes, ahead - modes, ahead)
        hit = jnp.abs(ahead) < 2 * REACH
        which = jnp.where(ahead < 0, 0, jnp.where(ahead > 0, 2, 1))
        slot = len(feeds)
        copy = pltpu.make_async_copy(ref["feed"].at[block, which], feed.at[slot], feed_sems.at[slot])
        pl.when(hit)(copy.start)
        feeds[stage, tile, block] = hit, copy, slot

    if fed:
        for tile in a_own:
            load_source(0, tile, 1)
            load_source(0, tile, 2)
        for tile in a_near:
            load_source(0, tile, 0)
            load_source(0, tile, 3)
        for tile in b:
            load_source(1, tile, 1)
            load_source(1, tile, 2)

    def add_source(target, lane, row, stage, tile, block, step):
        hit, copy, slot = feeds[stage, tile, block]

        @pl.when(hit)
        def _():
            copy.wait()

            def strip(i, _):
                at = pl.multiple_of(i * STRIP, STRIP)
                rows = pl.ds(pl.multiple_of(row + at, STRIP), STRIP)
                for c in range(HALVES):
                    target[lane + c, rows, :] = target[lane + c, rows, :] + step * feed[slot, c, pl.ds(at, STRIP), :]
                return 0

            lax.fori_loop(0, REACH // STRIP, strip, 0, unroll=8)

    out_copies = []

    def send(src, dst):
        copy = pltpu.make_async_copy(src, dst, out_sems.at[len(out_copies)])
        copy.start()
        out_copies.append(copy)

    def middle(tile, count, block):
        e_lane, m_lane = (tile - e_first) * HALVES, (tile - m_first) * HALVES

        def put(c, i, value, rate):
            rows = pl.ds(pl.multiple_of(block * REACH + i * STRIP, STRIP), STRIP)
            mid[m_lane + c, rows, :] = value + (0.5 * DT) * rate

        index = band_tiles.index(tile) * HALVES
        block_rates(win, e_lane, count, (block + 1) * REACH, coef, block * REACH, band, index, put)
        if fed:
            for d in range(count):
                add_source(mid, m_lane + d * HALVES, block * REACH, 0, tile + d, block, 0.5 * DT)

    def end(tile, count, block):
        e_lane, m_lane = (tile - e_first) * HALVES, (tile - m_first) * HALVES

        def put(c, i, value, rate):
            rows = pl.ds(pl.multiple_of((block + 1) * REACH + i * STRIP, STRIP), STRIP)
            win[e_lane + c, rows, :] = win[e_lane + c, rows, :] + DT * rate

        index = band_tiles.index(tile) * HALVES
        block_rates(mid, m_lane, count, block * REACH, coef, block * REACH, band, index, put)
        if fed:
            for d in range(count):
                add_source(win, e_lane + d * HALVES, (block + 1) * REACH, 1, tile + d, block, DT)

    wait(first)
    for tile, count in runs(a_own):
        middle(tile, count, 1)
        middle(tile, count, 2)
    for tile, out in zip(a_own, outs):
        send(mid.at[pair(tile - m_first), mid_rows, :], out)
    wait(second)
    for tile, count in runs(a_near):
        middle(tile, count, 0)
        middle(tile, count, 3)
    wait(third)
    for tile, count in runs(b):
        for block in (1, 2):
            end(tile, count, block)
            for c in range(count * HALVES):
                lane = pl.multiple_of((base + tile) * REACH + c * LANES, LANES)
                rows = pl.ds((block + 1) * REACH, REACH)
                dst = outs[-1].at[pl.ds((block - 1) * REACH, REACH), pl.ds(lane, LANES)]
                send(win.at[(tile - e_first) * HALVES + c, rows, :], dst)
    wait(out_copies)


def run_tiles(key, operands):
    names, a_own, a_near, b, own_loads, near_loads, far_loads, mid_loads, modes, fed, slab_shape = key
    tiles = [t for *_, t in own_loads + near_loads]
    e_first, e_count = min(tiles), max(tiles) - min(tiles) + 1
    tiles = sorted(set(a_own) | set(a_near) | {t + d for t in b for d in (-1, 0, 1)})
    m_first, m_count = tiles[0], tiles[-1] - tiles[0] + 1
    n_band = len(set(a_own) | set(a_near) | set(b))
    plan = key[:8] + (e_first, m_first, modes, slab_shape[1], fed)
    f32 = jnp.float32
    whole = pl.BlockSpec(memory_space=pl.ANY)
    shapes = [jax.ShapeDtypeStruct((HALVES, 2 * REACH, LANES), f32) for _ in a_own]
    if b:
        shapes.append(jax.ShapeDtypeStruct(slab_shape, f32))
    aliases = {names.index("prev"): len(a_own)} if "prev" in names else {}
    n_loads = HALVES * (len(own_loads) + len(near_loads) + len(far_loads)) + len(mid_loads) + n_band + 3
    n_feeds = 2 * (len(a_own) + len(a_near) + len(b)) if fed else 1
    work = 2 * (len(a_own) + len(a_near) + len(b)) * REACH * REACH
    return pl.pallas_call(
        functools.partial(tile_kernel, plan),
        out_shape=shapes,
        in_specs=[pl.BlockSpec(memory_space=pltpu.SMEM) if n == "base" else whole for n in names],
        out_specs=[whole] * len(shapes),
        scratch_shapes=[
            pltpu.VMEM((e_count * HALVES, 6 * REACH, LANES), f32),
            pltpu.VMEM((m_count * HALVES, 4 * REACH, LANES), f32),
            pltpu.VMEM((7, 4 * REACH, LANES), f32),
            pltpu.VMEM((n_band * HALVES, 7, STRIP, LANES), f32),
            pltpu.VMEM((n_feeds, HALVES, REACH, LANES), f32),
            pltpu.SemaphoreType.DMA((n_loads,)),
            pltpu.SemaphoreType.DMA((len(a_own) + 2 * HALVES * len(b),)),
            pltpu.SemaphoreType.DMA((n_feeds,)),
        ],
        input_output_aliases=aliases,
        compiler_params=pltpu.CompilerParams(vmem_limit_bytes=VMEM),
        cost_estimate=pl.CostEstimate(flops=28 * work, bytes_accessed=40 * work, transcendentals=0),
    )(*operands)


RUNS = {}


class Field:
    def __init__(self, slab, coef, band, feed, modes):
        self.slab, self.coef, self.band, self.feed, self.modes = slab, coef, band, feed, modes
        self.tiles = slab.shape[1] // REACH
        self.parts = {}
        self.mids = {}
        self.out = None
        self.last = None

    def step(self, base, a_own, a_near, b):
        operands = {"base": jnp.full((1,), base, jnp.int32)}
        own_loads, near_loads, far_loads, mid_loads = [], [], [], []
        for t in sorted({t + d for t in a_own for d in (-1, 0, 1)} | set(a_near) | set(b)):
            at = base + t
            if at < 0:
                name, value, place, from_base = "left", self.left, at + 2, False
            elif at >= self.tiles:
                name, value, place, from_base = "right", self.right, at - self.tiles, False
            else:
                name, value, place, from_base = "slab", self.slab, t, True
            operands[name] = value
            own_loads.append((name, place, from_base, t))

        def piece(kind, t):
            value, offset = self.parts[kind, base + t]
            name = f"{kind if value.shape[0] == 2 * REACH else kind[0]}{t}"
            operands[name] = value
            return kind, name, offset, t

        for t in sorted(set(a_own) | {t + d for t in a_near for d in (-1, 0, 1)}):
            near_loads += [piece(kind, t) for kind in ("PN", "QN")]
        for t in a_near:
            far_loads += [piece(kind, t) for kind in ("PF", "QF")]
        for t in sorted({t + d for t in b for d in (-1, 0, 1)} - set(a_own)):
            operands[f"M{t}"] = self.mids[base + t]
            mid_loads.append((f"M{t}", t))
        operands["coef"], operands["band"] = self.coef, self.band
        fed = self.feed is not None
        if fed:
            operands["feed"] = self.feed
        if b and self.out is not None:
            operands["prev"] = self.out
        loads = (tuple(own_loads), tuple(near_loads), tuple(far_loads), tuple(mid_loads))
        key = (tuple(operands), tuple(a_own), tuple(a_near), tuple(b)) + loads
        key += (self.modes, fed, self.slab.shape)
        if key not in RUNS:
            RUNS[key] = jax.jit(functools.partial(run_tiles, key))
        results = RUNS[key](tuple(operands.values()))
        for t, value in zip(a_own, results):
            self.mids[base + t] = value
        if b:
            self.out = results[-1]
        self.last = results[0]


def shards(g_start, cotangent, damping, hopping, bonds, source):
    rows_dev, cols_dev = g_start.shape
    modes = damping.shape[0]
    n_row, n_col = lax.axis_size("row"), lax.axis_size("col")
    tiles = cols_dev // REACH
    assert rows_dev == 2 * REACH and cols_dev % REACH == 0 and tiles >= 3 and n_row % 2 == 0
    row_axis = lax.axis_index("row")
    odd = lax.rem(row_axis, 2)
    row_first = row_axis * rows_dev
    col_first = lax.axis_index("col") * cols_dev

    def ring(array, first, count):
        extra = 2 * REACH
        array = jnp.concatenate([array[:, modes - extra :], array, array[:, :extra]], axis=1)
        return lax.dynamic_slice_in_dim(array, first + extra, count, 1)

    def gathered(first, count):
        wide = count + 2 * REACH
        damp = ring(damping[None, :], first - REACH, wide)
        hop = ring(hopping, first - REACH, wide)
        bond = ring(bonds, first - REACH, wide).astype(jnp.float32)
        coef = jnp.concatenate([-damp, hop], axis=0) * bond
        turned = [coef[m, REACH + o : REACH + o + count] for m, o in zip(MIRROR, OFFSETS)]
        return coef[:, REACH : REACH + count], jnp.stack(turned)

    count = 4 * REACH
    inside = row_first - REACH + lax.iota(jnp.int32, count)
    inside = (inside >= 0) & (inside < n_row * rows_dev)
    feed = jnp.where(inside[None, :], ring(source, row_first - REACH, count), 0.0)
    shape = (4, 3, HALVES, REACH, LANES)
    axis = functools.partial(lax.broadcasted_iota, jnp.int32, shape)
    rel = (axis(1) - 1) * REACH + axis(2) * LANES + axis(4) - axis(3)
    dense = jnp.zeros(shape, jnp.float32)
    for k, offset in enumerate(OFFSETS):
        dense = dense + jnp.where(rel == offset, feed[k].reshape(4, 1, 1, REACH, 1), 0.0)
    row_coefs = gathered(row_first - REACH, count)
    col_coefs = gathered(col_first - REACH, cols_dev + 2 * REACH)

    def row_table(coef):
        coef = jnp.where(inside[None, :], coef, 0.0)
        return jnp.broadcast_to(coef[:, :, None], (7, count, LANES))

    def col_table(coef):
        coef = coef.reshape(7, (tiles + 2) * HALVES, 1, LANES).transpose(1, 0, 2, 3)
        return jnp.broadcast_to(coef, ((tiles + 2) * HALVES, 7, STRIP, LANES))

    fields = [
        Field(slab, row_table(row), col_table(col), fed, modes)
        for slab, row, col, fed in zip((g_start, cotangent), row_coefs, col_coefs, (dense, None))
    ]

    swap = [(i, i ^ 1) for i in range(n_row)]
    relay = [(i, i + 2) for i in range(0, n_row - 2, 2)] + [(i, i - 2) for i in range(3, n_row, 2)]
    to_right = [(i, (i + 1) % n_col) for i in range(n_col)]
    to_left = [((i + 1) % n_col, i) for i in range(n_col)]

    swapped, relayed = [], []
    holds = {}

    def after(value, others):
        others = [other for other in others if other is not None]
        if not others:
            return value
        return lax.optimization_barrier((value, *others))[0]

    def exchange(field, tile, halves):
        pieces = []
        for half in halves:
            start = (odd if half == 0 else 1 - odd) * REACH
            for c in range(HALVES):
                at = (start, tile * REACH + c * LANES)
                pieces.append(lax.dynamic_slice(field.slab, at, (REACH, LANES)))
        piece = jnp.concatenate(pieces, axis=0)
        index = len(swapped)
        earlier = swapped[index - IN_FLIGHT] if index >= IN_FLIGHT else None
        got = lax.ppermute(after(piece, [earlier, holds.pop(index, None)]), "row", swap)
        earlier = relayed[index - IN_FLIGHT] if index >= IN_FLIGHT else None
        passed = lax.ppermute(after(got, [earlier]), "row", relay)
        swapped.append(got)
        relayed.append(passed)
        for place, half in enumerate(halves):
            field.parts["PN" if half else "PF", tile] = got, place * HALVES
            field.parts["QF" if half else "QN", tile] = passed, place * HALVES

    def edge(field, source_tile, target_tile, route):
        for kinds in (("PF", "PN"), ("QN", "QF")):
            moved = lax.ppermute(field.parts[kinds[0], source_tile][0], "col", route)
            for place, kind in enumerate(kinds):
                field.parts[kind, target_tile] = moved, place * HALVES

    for field in fields:

        def step(*args, field=field):
            field.step(*args)
            holds[len(swapped) - 1 + HOLD] = field.last

        field.left = lax.ppermute(field.slab[:, cols_dev - 2 * REACH :], "col", to_right)
        field.right = lax.ppermute(field.slab[:, : 2 * REACH], "col", to_left)
        last = tiles - 2
        exchange(field, 0, (0, 1))
        edge(field, 0, tiles, to_left)
        exchange(field, tiles - 1, (0, 1))
        edge(field, tiles - 1, -1, to_right)
        step(0, (-1, 0), (), ())
        for tile in range(1, last):
            exchange(field, tile, (0, 1))
            if tile % 2 == 0:
                step(tile, (-1, 0), (-2, -1), (-2, -1))
            elif tile == last - 1:
                step(tile, (0,), (-1,), (-1,))
        exchange(field, last, (0,))
        exchange(field, last, (1,))
        step(last, (1, 2), (), ())
        step(last, (0,), (-1, 1), (-1, 1))
        step(last, (), (0,), (0,))
    return tuple(field.out for field in fields)


def solution(mesh):
    return jax.shard_map(
        shards,
        mesh=mesh,
        in_specs=(P("row", "col"), P("row", "col"), P(), P(), P(), P()),
        out_specs=(P("row", "col"), P("row", "col")),
        check_vma=False,
    )
```

```python
import functools

import jax
import jax.numpy as jnp
from jax import lax
from jax.experimental import pallas as pl
from jax.experimental.pallas import tpu as pltpu
from jax.sharding import PartitionSpec as P

LX = 128
DT = 0.1

LANES = 128
STRIP = 8
REACH = 2 * LX
HALVES = REACH // LANES
UNROLL = 64
OFFSETS = (0, 1, -1, 2, -2, REACH, -REACH)
MIRROR = (0, 2, 1, 4, 3, 6, 5)
IN_FLIGHT = 2
DEFER = 1
RELAYS = 2
HOLD = 5
VMEM = 24 * 2**20


def block_rates(win, lane, count, row, coef, coef_row, band, index, put):
    lanes = lax.broadcasted_iota(jnp.int32, (STRIP, LANES), 1)
    wide = count * HALVES

    def strip(i, _):
        at = pl.multiple_of(row + i * STRIP, STRIP)
        rows_c = pl.ds(pl.multiple_of(coef_row + i * STRIP, STRIP), STRIP)
        weights = [coef[k, rows_c, :] for k in range(7)]

        def load(j, shift=0):
            return win[lane + j, pl.ds(at + shift, STRIP), :]

        line = [load(j) for j in range(-1, wide + 1)]

        def moved(shift):
            if shift > 0:
                turned = [pltpu.roll(v, LANES - shift, 1) for v in line[1:]]
                return [jnp.where(lanes < LANES - shift, turned[c], turned[c + 1]) for c in range(wide)]
            turned = [pltpu.roll(v, -shift, 1) for v in line[:-1]]
            return [jnp.where(lanes >= -shift, turned[c + 1], turned[c]) for c in range(wide)]

        by_col = {s: moved(s) for s in (1, -1, 2, -2)}
        by_col[REACH] = [load(c + HALVES) for c in range(wide)]
        by_col[-REACH] = [load(c - HALVES) for c in range(wide)]
        for c in range(wide):
            value = line[c + 1]
            total = (weights[0] + band[index + c, 0]) * value
            for k in range(1, 7):
                total = total + weights[k] * load(c, OFFSETS[k])
                total = total + band[index + c, k] * by_col[OFFSETS[k]][c]
            put(c, i, value, total)
        return 0

    lax.fori_loop(0, REACH // STRIP, strip, 0, unroll=max(UNROLL // wide, 1))


def runs(tiles):
    found = []
    for tile in tiles:
        if found and tile == found[-1][0] + found[-1][1]:
            found[-1] = (found[-1][0], found[-1][1] + 1)
        else:
            found.append((tile, 1))
    return found


def tile_kernel(plan, *refs):
    names, a_own, a_near, b, own_loads, near_loads, far_loads, mid_loads, e_first, m_first, modes, cols, fed = plan
    n_in, n_out = len(names), len(a_own) + (1 if b else 0)
    ref = dict(zip(names, refs[:n_in]))
    outs = refs[n_in : n_in + n_out]
    coef = ref["coef"]
    win, mid, band, feed, sems, out_sems, feed_sems = refs[n_in + n_out :]
    base = ref["base"][0]
    row_axis = lax.axis_index("row")
    odd = lax.rem(row_axis, 2)
    block_of = {"PF": 5 - 5 * odd, "PN": 4 - 3 * odd, "QN": 1 + 3 * odd, "QF": 5 * odd}
    half_of = {"PF": 1 - odd, "PN": odd, "QN": 1 - odd, "QF": odd}
    row_first = row_axis * (2 * REACH)
    col_first = lax.axis_index("col") * cols
    own_rows = pl.ds(2 * REACH, 2 * REACH)
    mid_rows = pl.ds(REACH, 2 * REACH)
    used = []

    def load(src, dst):
        copy = pltpu.make_async_copy(src, dst, sems.at[len(used)])
        copy.start()
        used.append(copy)
        return copy

    def pair(first):
        return pl.ds(first * HALVES, HALVES)

    def load_piece(kind, name, full, tile, group):
        start = pl.multiple_of(block_of[kind] * REACH, REACH)
        at = pl.multiple_of(half_of[kind] * REACH, REACH) if full else 0
        for c in range(HALVES):
            src = ref[name].at[pl.ds(at, REACH), pl.ds(c * LANES, LANES)]
            group.append(load(src, win.at[(tile - e_first) * HALVES + c, pl.ds(start, REACH), :]))

    band_tiles = sorted(set(a_own) | set(a_near) | set(b))
    first, second, third = [], [], []
    for name, at, from_base, tile in own_loads:
        for c in range(HALVES):
            lane = at * REACH + c * LANES
            if from_base:
                lane = pl.multiple_of(base * REACH + lane, LANES)
            src = ref[name].at[:, pl.ds(lane, LANES)]
            first.append(load(src, win.at[(tile - e_first) * HALVES + c, own_rows, :]))
    for index, tile in enumerate(band_tiles):
        src = ref["band"].at[pl.ds((base + tile + 1) * HALVES, HALVES)]
        first.append(load(src, band.at[pair(index)]))
    for kind, name, full, tile in near_loads:
        load_piece(kind, name, full, tile, first if tile in a_own else second)
    for kind, name, full, tile in far_loads:
        load_piece(kind, name, full, tile, second)
    for name, tile in mid_loads:
        third.append(load(ref[name], mid.at[pair(tile - m_first), mid_rows, :]))

    def wait(copies):
        for copy in copies:
            copy.wait()

    feeds = {}

    def load_source(stage, tile, block):
        ahead = col_first + (base + tile) * REACH - (row_first + (block - 1) * REACH)
        ahead = lax.rem(ahead + 2 * modes, modes)
        ahead = jnp.where(ahead * 2 > modes, ahead - modes, ahead)
        hit = jnp.abs(ahead) < 2 * REACH
        which = jnp.where(ahead < 0, 0, jnp.where(ahead > 0, 2, 1))
        slot = len(feeds)
        copy = pltpu.make_async_copy(ref["feed"].at[block, which], feed.at[slot], feed_sems.at[slot])
        pl.when(hit)(copy.start)
        feeds[stage, tile, block] = hit, copy, slot

    if fed:
        for tile in a_own:
            load_source(0, tile, 1)
            load_source(0, tile, 2)
        for tile in a_near:
            load_source(0, tile, 0)
            load_source(0, tile, 3)
        for tile in b:
            load_source(1, tile, 1)
            load_source(1, tile, 2)

    def add_source(target, lane, row, stage, tile, block, step):
        hit, copy, slot = feeds[stage, tile, block]

        @pl.when(hit)
        def _():
            copy.wait()

            def strip(i, _):
                at = pl.multiple_of(i * STRIP, STRIP)
                rows = pl.ds(pl.multiple_of(row + at, STRIP), STRIP)
                for c in range(HALVES):
                    target[lane + c, rows, :] = target[lane + c, rows, :] + step * feed[slot, c, pl.ds(at, STRIP), :]
                return 0

            lax.fori_loop(0, REACH // STRIP, strip, 0, unroll=8)

    out_copies = []

    def send(src, dst):
        copy = pltpu.make_async_copy(src, dst, out_sems.at[len(out_copies)])
        copy.start()
        out_copies.append(copy)

    def middle(tile, count, block):
        e_lane, m_lane = (tile - e_first) * HALVES, (tile - m_first) * HALVES

        def put(c, i, value, rate):
            rows = pl.ds(pl.multiple_of(block * REACH + i * STRIP, STRIP), STRIP)
            mid[m_lane + c, rows, :] = value + (0.5 * DT) * rate

        index = band_tiles.index(tile) * HALVES
        block_rates(win, e_lane, count, (block + 1) * REACH, coef, block * REACH, band, index, put)
        if fed:
            for d in range(count):
                add_source(mid, m_lane + d * HALVES, block * REACH, 0, tile + d, block, 0.5 * DT)

    def end(tile, count, block):
        e_lane, m_lane = (tile - e_first) * HALVES, (tile - m_first) * HALVES

        def put(c, i, value, rate):
            rows = pl.ds(pl.multiple_of((block + 1) * REACH + i * STRIP, STRIP), STRIP)
            win[e_lane + c, rows, :] = win[e_lane + c, rows, :] + DT * rate

        index = band_tiles.index(tile) * HALVES
        block_rates(mid, m_lane, count, block * REACH, coef, block * REACH, band, index, put)
        if fed:
            for d in range(count):
                add_source(win, e_lane + d * HALVES, (block + 1) * REACH, 1, tile + d, block, DT)

    wait(first)
    for tile, count in runs(a_own):
        middle(tile, count, 1)
        middle(tile, count, 2)
    for tile, out in zip(a_own, outs):
        send(mid.at[pair(tile - m_first), mid_rows, :], out)
    wait(second)
    for tile, count in runs(a_near):
        middle(tile, count, 0)
        middle(tile, count, 3)
    wait(third)
    for tile, count in runs(b):
        for block in (1, 2):
            end(tile, count, block)
            for c in range(count * HALVES):
                lane = pl.multiple_of((base + tile) * REACH + c * LANES, LANES)
                rows = pl.ds((block + 1) * REACH, REACH)
                dst = outs[-1].at[pl.ds((block - 1) * REACH, REACH), pl.ds(lane, LANES)]
                send(win.at[(tile - e_first) * HALVES + c, rows, :], dst)
    wait(out_copies)


def run_tiles(key, operands):
    names, a_own, a_near, b, own_loads, near_loads, far_loads, mid_loads, modes, fed, slab_shape = key
    tiles = [t for *_, t in own_loads + near_loads]
    e_first, e_count = min(tiles), max(tiles) - min(tiles) + 1
    tiles = sorted(set(a_own) | set(a_near) | {t + d for t in b for d in (-1, 0, 1)})
    m_first, m_count = tiles[0], tiles[-1] - tiles[0] + 1
    n_band = len(set(a_own) | set(a_near) | set(b))
    plan = key[:8] + (e_first, m_first, modes, slab_shape[1], fed)
    f32 = jnp.float32
    whole = pl.BlockSpec(memory_space=pl.ANY)
    places = {"base": pl.BlockSpec(memory_space=pltpu.SMEM), "coef": pl.BlockSpec(memory_space=pltpu.VMEM)}
    operands = [
        v if n == "base" else pltpu.with_memory_space_constraint(v, pltpu.VMEM if n == "coef" else pltpu.HBM)
        for n, v in zip(names, operands)
    ]
    shapes = [jax.ShapeDtypeStruct((HALVES, 2 * REACH, LANES), f32) for _ in a_own]
    if b:
        shapes.append(jax.ShapeDtypeStruct(slab_shape, f32))
    aliases = {names.index("prev"): len(a_own)} if "prev" in names else {}
    n_loads = HALVES * (len(own_loads) + len(near_loads) + len(far_loads)) + len(mid_loads) + n_band + 3
    n_feeds = 2 * (len(a_own) + len(a_near) + len(b)) if fed else 1
    work = 2 * (len(a_own) + len(a_near) + len(b)) * REACH * REACH
    return pl.pallas_call(
        functools.partial(tile_kernel, plan),
        out_shape=shapes,
        in_specs=[places.get(n, whole) for n in names],
        out_specs=[whole] * len(shapes),
        scratch_shapes=[
            pltpu.VMEM((e_count * HALVES, 6 * REACH, LANES), f32),
            pltpu.VMEM((m_count * HALVES, 4 * REACH, LANES), f32),
            pltpu.VMEM((n_band * HALVES, 7, STRIP, LANES), f32),
            pltpu.VMEM((n_feeds, HALVES, REACH, LANES), f32),
            pltpu.SemaphoreType.DMA((n_loads,)),
            pltpu.SemaphoreType.DMA((len(a_own) + 2 * HALVES * len(b),)),
            pltpu.SemaphoreType.DMA((n_feeds,)),
        ],
        input_output_aliases=aliases,
        compiler_params=pltpu.CompilerParams(vmem_limit_bytes=VMEM),
        cost_estimate=pl.CostEstimate(flops=28 * work, bytes_accessed=40 * work, transcendentals=0),
    )(*operands)


RUNS = {}


class Field:
    def __init__(self, slab, modes):
        self.slab, self.modes, self.feed = slab, modes, None
        self.tiles = slab.shape[1] // REACH
        self.parts = {}
        self.mids = {}
        self.out = None
        self.last = None

    def step(self, base, a_own, a_near, b, since):
        operands = {"base": lax.optimization_barrier((jnp.full((1,), base, jnp.int32), since))[0]}
        own_loads, near_loads, far_loads, mid_loads = [], [], [], []
        for t in sorted({t + d for t in a_own for d in (-1, 0, 1)} | set(a_near) | set(b)):
            at = base + t
            if at < 0:
                name, value, place, from_base = "left", self.left, at + 2, False
            elif at >= self.tiles:
                name, value, place, from_base = "right", self.right, at - self.tiles, False
            else:
                name, value, place, from_base = "slab", self.slab, t, True
            operands[name] = value
            own_loads.append((name, place, from_base, t))

        def piece(kind, t):
            value = self.parts[kind, base + t]
            full = value.shape[0] == 2 * REACH
            name = f"{kind[0] if full else kind}{t}"
            operands[name] = value
            return kind, name, full, t

        for t in sorted(set(a_own) | {t + d for t in a_near for d in (-1, 0, 1)}):
            near_loads += [piece(kind, t) for kind in ("PN", "QN")]
        for t in a_near:
            far_loads += [piece(kind, t) for kind in ("PF", "QF")]
        for t in sorted({t + d for t in b for d in (-1, 0, 1)} - set(a_own)):
            operands[f"M{t}"] = self.mids[base + t]
            mid_loads.append((f"M{t}", t))
        operands["coef"], operands["band"] = self.coef, self.band
        fed = self.feed is not None
        if fed:
            operands["feed"] = self.feed
        if b and self.out is not None:
            operands["prev"] = self.out
        loads = (tuple(own_loads), tuple(near_loads), tuple(far_loads), tuple(mid_loads))
        key = (tuple(operands), tuple(a_own), tuple(a_near), tuple(b)) + loads
        key += (self.modes, fed, self.slab.shape)
        if key not in RUNS:
            RUNS[key] = jax.jit(functools.partial(run_tiles, key))
        results = RUNS[key](tuple(operands.values()))
        for t, value in zip(a_own, results):
            self.mids[base + t] = value
        if b:
            self.out = results[-1]
        self.last = results[-1]


def shards(g_start, cotangent, damping, hopping, bonds, source):
    rows_dev, cols_dev = g_start.shape
    modes = damping.shape[0]
    n_row, n_col = lax.axis_size("row"), lax.axis_size("col")
    tiles = cols_dev // REACH
    assert rows_dev == 2 * REACH and cols_dev % (2 * REACH) == 0 and tiles >= 4 and n_row % 2 == 0
    row_axis = lax.axis_index("row")
    odd = lax.rem(row_axis, 2)
    row_first = row_axis * rows_dev
    col_first = lax.axis_index("col") * cols_dev

    def ring(array, first, count):
        extra = 2 * REACH
        array = jnp.concatenate([array[:, modes - extra :], array, array[:, :extra]], axis=1)
        return lax.dynamic_slice_in_dim(array, first + extra, count, 1)

    def gathered(first, count):
        wide = count + 2 * REACH
        damp = ring(damping[None, :], first - REACH, wide)
        hop = ring(hopping, first - REACH, wide)
        bond = ring(bonds, first - REACH, wide).astype(jnp.float32)
        coef = jnp.concatenate([-damp, hop], axis=0) * bond
        turned = [coef[m, REACH + o : REACH + o + count] for m, o in zip(MIRROR, OFFSETS)]
        return coef[:, REACH : REACH + count], jnp.stack(turned)

    swap = [(i, i ^ 1) for i in range(n_row)]
    relay = [(i, i + 2) for i in range(0, n_row - 2, 2)] + [(i, i - 2) for i in range(3, n_row, 2)]
    to_right = [(i, (i + 1) % n_col) for i in range(n_col)]
    to_left = [((i + 1) % n_col, i) for i in range(n_col)]

    fields = [Field(slab, modes) for slab in (g_start, cotangent)]
    swapped, relayed = [], []
    holds, relay_holds = {}, {}

    def after(value, *others):
        others = [other for other in others if other is not None]
        if not others:
            return value
        return lax.optimization_barrier((value, *others))[0]

    def past(chain, index, lag):
        return chain[index - lag] if index >= lag else None

    def exchange(field, tile, half=None):
        index = len(swapped)
        slab = field.slab if field is fields[0] else after(field.slab, swapped[0])
        if half is None:
            piece = slab[:, tile * REACH : (tile + 1) * REACH]
        else:
            start = (odd if half == 0 else 1 - odd) * REACH
            piece = lax.dynamic_slice(slab, (start, tile * REACH), (REACH, REACH))
        got = lax.ppermute(after(piece, past(swapped, index, IN_FLIGHT), *holds.pop(index, ())), "row", swap)
        passed = lax.ppermute(after(got, past(relayed, index, RELAYS), *relay_holds.pop(index, ())), "row", relay)
        swapped.append(got)
        relayed.append(passed)
        for kind, of_half, value in (("PF", 0, got), ("PN", 1, got), ("QN", 0, passed), ("QF", 1, passed)):
            if half in (None, of_half):
                field.parts[kind, tile] = value

    def step(field, *args, lag=HOLD):
        field.step(*args, swapped[-1])
        index = len(swapped) - 1
        if index + lag < len(pieces):
            holds.setdefault(index + lag, []).append(field.last)
        elif index + 2 < len(pieces):
            relay_holds.setdefault(index + 2, []).append(field.last)

    raw = (damping, hopping, bonds, source)

    def prepare():
        damping, hopping, bonds, source = lax.optimization_barrier((*raw, swapped[0]))[:4]
        count = 4 * REACH
        inside = row_first - REACH + lax.iota(jnp.int32, count)
        inside = (inside >= 0) & (inside < n_row * rows_dev)
        feed = jnp.where(inside[None, :], ring(source, row_first - REACH, count), 0.0)
        shape = (4, 3, HALVES, REACH, LANES)
        axis = functools.partial(lax.broadcasted_iota, jnp.int32, shape)
        rel = (axis(1) - 1) * REACH + axis(2) * LANES + axis(4) - axis(3)
        dense = jnp.zeros(shape, jnp.float32)
        for k, offset in enumerate(OFFSETS):
            dense = dense + jnp.where(rel == offset, feed[k].reshape(4, 1, 1, REACH, 1), 0.0)
        row_coefs = gathered(row_first - REACH, count)
        col_coefs = gathered(col_first - REACH, cols_dev + 2 * REACH)

        def row_table(coef):
            coef = jnp.where(inside[None, :], coef, 0.0)
            return jnp.broadcast_to(coef[:, :, None], (7, count, LANES))

        def col_table(coef):
            coef = coef.reshape(7, (tiles + 2) * HALVES, 1, LANES).transpose(1, 0, 2, 3)
            return jnp.broadcast_to(coef, ((tiles + 2) * HALVES, 7, STRIP, LANES))

        for field, row, col in zip(fields, row_coefs, col_coefs):
            field.coef, field.band = row_table(row), col_table(col)
        fields[0].feed = dense


    forward, adjoint = fields
    last = tiles - 2

    def side(field, right):
        route, name = (to_right, "left") if right else (to_left, "right")
        first = cols_dev - 2 * REACH if right else 0

        def send():
            slab = after(field.slab, swapped[0])
            setattr(field, name, lax.ppermute(after(slab[:, first : first + 2 * REACH], swapped[-1]), "col", route))

        return send

    def edge(field, kind, right):
        source_tile, target_tile, route = (tiles - 1, -1, to_right) if right else (0, tiles, to_left)

        def send():
            value = after(field.parts[kind, source_tile], swapped[-1])
            field.parts[kind, target_tile] = lax.ppermute(value, "col", route)

        return send

    def call(*args, **kwargs):
        return lambda: step(*args, **kwargs)

    pieces = []
    extra = [(forward, 0), (forward, tiles - 1), (adjoint, 0), (adjoint, tiles - 1)]
    for tile in range(1, last + 1):
        work = []
        if tile == 2:
            work = [call(forward, 2, (-1, 0), (), ())]
        elif tile % 2 == 0:
            work = [call(forward, tile, (-1, 0), (-2, -1), (-2, -1))]
        pieces.append((forward, tile, None, work))
        if tile % 2 == 0 and extra:
            pieces.append((*extra.pop(0), None, []))
    pieces += [(*one, None, []) for one in extra]
    for tile in range(1, last):
        work = []
        if tile == last - 1:
            work = [call(adjoint, tile, (0,), (-1,), (-1,))]
        elif tile % 2 == 0:
            work = [call(adjoint, tile, (-1, 0), (-2, -1), (-2, -1))]
        pieces.append((adjoint, tile, None, work))
    pieces.append((adjoint, last, 0, []))
    pieces.append(
        (adjoint, last, 1, [call(adjoint, last, (0,), (-1, 1), (-1, 1)), call(adjoint, last, (), (0,), (0,))])
    )
    sides = [side(forward, True), side(forward, False)]
    sides += [edge(forward, kind, right) for right in (False, True) for kind in ("PN", "QN")]
    sides += [side(adjoint, True), side(adjoint, False)]
    sides += [edge(adjoint, kind, right) for right in (False, True) for kind in ("PN", "QN")]
    ends = [place for place, one in enumerate(pieces) if one[0] is forward and one[1] == last][0]
    late = [
        (4, 6, call(forward, 1, (-2, -1), (-1, 0), (-1, 0))),
        (ends, 6, call(forward, last, (1, 2), (0, 1), (0, 1))),
        (0, 12, call(adjoint, 0, (-1, 0), (), ())),
        (0, 12, call(adjoint, tiles - 1, (0, 1), (), ())),
    ]

    def needs(index):
        owner = {2: 0, 3: 0, 4: 1, 5: 1, 8: 2, 9: 2, 10: 3, 11: 3}.get(index)
        if owner is None:
            return 0
        field, tile = [(forward, 0), (forward, tiles - 1), (adjoint, 0), (adjoint, tiles - 1)][owner]
        return [place for place, one in enumerate(pieces) if one[:2] == (field, tile)][0] + 1

    count_sent = 0
    waiting = []
    few = tiles < 8
    for place, (field, tile, half, work) in enumerate(pieces):
        exchange(field, tile, half)
        if place == 0:
            prepare()
        while count_sent < len(sides) and place >= needs(count_sent):
            sides[count_sent]()
            count_sent += 1
            if place < len(pieces) - 4 and not few:
                break
        final = place == len(pieces) - 1
        waiting += [(place + DEFER, one) for one in work]
        outer = [one for one in late if place > one[0] + DEFER and count_sent >= one[1]]
        due = [one for one in waiting if final or one[0] <= place]
        if not final and not few:
            outer = [] if due else outer[:1]
        for one in outer:
            one[2]()
            late.remove(one)
        for one in due:
            one[1]()
            waiting.remove(one)
    return tuple(field.out for field in fields)


def solution(mesh):
    return jax.shard_map(
        shards,
        mesh=mesh,
        in_specs=(P("row", "col"), P("row", "col"), P(), P(), P(), P()),
        out_specs=(P("row", "col"), P("row", "col")),
        check_vma=False,
    )
```
